32 devices in a mesh: mol: 2 (over x), term: 16 (over z, y, core).
Axes of the slice: x: 2, y: 2, z: 4, core: 2. Of those that a mesh axis runs over, the one named last changes fastest.
Arguments:
- wave: bfloat16 [32, 2, 256, 256], P(('mol', 'term')), parts along dimension 0, may hold values from -6 to 6
- left_ops: bfloat16 [64, 24, 256, 256], P(('mol', 'term')), parts along dimension 0, may hold values from -0.375 to 0.375
- right_ops: bfloat16 [64, 24, 256, 256], P(('mol', 'term')), parts along dimension 0, may hold values from -0.375 to 0.375
- pair_src: int32 [64, 24], P(('mol', 'term')), parts along dimension 0, may hold values from 0 to 15
- pair_dst: int32 [64, 24], P(('mol', 'term')), parts along dimension 0, may hold values from 0 to 15
- sector_dims: int32 [2, 32], P(None, 'mol'), parts along dimension 1, may hold values from 128 to 256
Outputs:
- product: bfloat16 [32, 2, 256, 256], P(('mol', 'term')), parts along dimension 0
The draws below stay inside these ranges and needn't reach their ends.
There are 2 independent parts, one for each index of `mol`. The reference program is written for one: setup_inputs(seed, part) draws one part's arguments, and reference() takes and returns one part's arrays. A program takes and returns all parts, laid end to end along the dimension named above; each array names one. Nothing has to cross between parts.
All inputs are finite; a program needn't handle non-finite values.
Results may differ from the reference program's by a relative error of at most 0.0049.
Values may be sent and summed in bfloat16 or wider, within the bound.
A program may use at most 128 MiB of HBM per device.

```python
import jax
import jax.numpy as jnp
from jax import lax

B = 256
NV = 2
PAIRS = 24
TERMS = 32
SECTORS = 16


def place_ends(entries, own_key, smallest, largest):
    longest = entries.shape.index(max(entries.shape))
    spots = []
    for shift in (0, 1):
        where = [jax.random.randint(jax.random.fold_in(own_key, axis), (), 0, length) for axis, length in enumerate(entries.shape)]
        where[longest] = (where[longest] + shift) % entries.shape[longest]
        spots.append(tuple(where))
    return entries.at[spots[0]].set(smallest).at[spots[1]].set(largest)


def levels(rng, extent, pieces, low, top_value):
    def one(position, shards_of):
        heights = jax.random.uniform(jax.random.fold_in(jax.random.fold_in(rng, 6), position), (shards_of,), jnp.float32, low / len(pieces), top_value / len(pieces))
        return jnp.repeat(jnp.exp(heights), extent[position] // shards_of).reshape((-1,) + (1,) * (len(extent) - position - 1))

    gain = one(*pieces[0])
    for cut in pieces[1:]:
        gain = gain * one(*cut)
    return gain


def gaussian(own_key, shape, scale, limit, shards=(), held_as=jnp.bfloat16):
    loudness = levels(own_key, shape, shards, -0.22, 0.18) if shards else 1.0
    values = jax.random.normal(own_key, shape, jnp.float32) * scale * loudness
    return jnp.minimum(jnp.maximum(values, -limit), limit).astype(held_as)


def setup_inputs(seed: int = 0, part: int = 0) -> dict:
    streams_of = jax.random.split(jax.random.key(seed), 7)
    part_splits = jax.random.split(jax.random.fold_in(streams_of[6], part), 7)
    return {
        "wave": gaussian(part_splits[0], (SECTORS, NV, B, B), 1.0, 6.0, ((0, 16),)),
        "left_ops": gaussian(part_splits[1], (TERMS, PAIRS, B, B), B ** -0.5, 0.375, ((0, 16),)),
        "right_ops": gaussian(part_splits[2], (TERMS, PAIRS, B, B), B ** -0.5, 0.375, ((0, 16),)),
        "pair_src": place_ends(jax.random.randint(part_splits[3], (TERMS, PAIRS), 0, SECTORS), jax.random.fold_in(part_splits[3], 1), 0, SECTORS - 1).astype(jnp.int32),
        "pair_dst": place_ends(jax.random.randint(part_splits[4], (TERMS, PAIRS), 0, SECTORS), jax.random.fold_in(part_splits[4], 1), 0, SECTORS - 1).astype(jnp.int32),
        "sector_dims": place_ends(jax.random.randint(part_splits[5], (2, SECTORS), B // 2, B + 1), jax.random.fold_in(part_splits[5], 1), B // 2, B).astype(jnp.int32),
    }


def sector_mask(sector_dims, size):
    rows = jnp.arange(size, dtype=jnp.int32)
    row_ok = (rows[None, :] < sector_dims[0][:, None]).astype(jnp.float32)
    col_ok = (rows[None, :] < sector_dims[1][:, None]).astype(jnp.float32)
    return row_ok[:, :, None] * col_ok[:, None, :]


def reference(wave, left_ops, right_ops, pair_src, pair_dst, sector_dims):
    mask = sector_mask(sector_dims, B)
    masked = (wave.astype(jnp.float32) * mask[:, None]).astype(jnp.bfloat16)
    lefts = left_ops.reshape(TERMS * PAIRS, B, B)
    rights = right_ops.reshape(TERMS * PAIRS, B, B)
    srcs = pair_src.reshape(-1).astype(jnp.int32)
    dsts = pair_dst.reshape(-1).astype(jnp.int32)

    def step(total, items):
        left, right, src, dst = items
        block = masked[src]
        half = jnp.einsum("ij,vjk->vik", left.astype(jnp.float32), block.astype(jnp.float32)).astype(jnp.bfloat16)
        full = jnp.einsum("vik,lk->vil", half.astype(jnp.float32), right.astype(jnp.float32))
        return total.at[dst].add(full), None

    start = jnp.zeros((SECTORS, NV, B, B), jnp.float32)
    total, _ = lax.scan(step, start, (lefts, rights, srcs, dsts))
    return (total * mask[:, None]).astype(jnp.bfloat16)
```

```python
import functools

import jax
import jax.numpy as jnp
from jax import lax
from jax.experimental import pallas as pl
from jax.experimental.pallas import tpu as pltpu
from jax.sharding import PartitionSpec as P

MESH = pl.DeviceIdType.MESH
GROUP = 4


def chip_of(pos, chips):
    if chips == 8:
        back = pos // 4
        return 2 * (pos + back * (7 - 2 * pos)) + back
    return pos


def pos_of(chip, chips):
    if chips == 8:
        up, col = chip // 2, chip % 2
        return up + col * (7 - 2 * up)
    return chip


def places(chips):
    me = lax.axis_index("term")
    core = lax.rem(me, 2)
    pos = pos_of(me // 2, chips)

    def at(shift):
        return 2 * chip_of(lax.rem(pos + shift + chips, chips), chips) + core

    return me, core, at, me + 1 - 2 * core


def mask_of(dims_ref, sector, size):
    rows = lax.broadcasted_iota(jnp.int32, (size, size), 0)
    cols = lax.broadcasted_iota(jnp.int32, (size, size), 1)
    inside = (rows < dims_ref[0, sector]) & (cols < dims_ref[1, sector])
    return jnp.where(inside, 1.0, 0.0).astype(jnp.float32)


def greet(devices):
    barrier = pltpu.get_barrier_semaphore()
    for device in devices:
        pl.semaphore_signal(barrier, inc=1, device_id={"term": device}, device_id_type=MESH)
    pl.semaphore_wait(barrier, len(devices))


def reach(chips, way, v):
    return chips // 2 - (1 if way != v else 0)


def gather_kernel(chips, dims_ref, wave_ref, out_ref, own, local_sem, ring_send, ring_recv, sib_send, sib_recv):
    size = wave_ref.shape[-1]
    me, core, at, sib = places(chips)
    flip = 1 - 2 * core
    greet((at(1), at(-1), sib))
    mask = mask_of(dims_ref, me, size)
    waits = []
    half = chips // 2

    def ring(way, step, v, src, index):
        return pltpu.make_async_remote_copy(
            src_ref=src,
            dst_ref=out_ref.at[index, v],
            send_sem=ring_send.at[way, step, v],
            recv_sem=ring_recv.at[way, step, v],
            device_id={"term": at(1 - 2 * way)},
            device_id_type=MESH,
        )

    def sibling(way, step, v, src, index):
        return pltpu.make_async_remote_copy(
            src_ref=src,
            dst_ref=out_ref.at[index, v],
            send_sem=sib_send.at[way, step, v],
            recv_sem=sib_recv.at[way, step, v],
            device_id={"term": sib},
            device_id_type=MESH,
        )

    for v in range(2):
        own[v] = (wave_ref[0, v].astype(jnp.float32) * mask).astype(jnp.bfloat16)
        for way in range(2):
            copy = ring(way, 0, v, own.at[v], me)
            copy.start()
            waits.append(copy)
    for v in range(2):
        copy = sibling(0, half, v, own.at[v], me)
        copy.start()
        waits.append(copy)
        copy = pltpu.make_async_copy(own.at[v], out_ref.at[me, v], local_sem.at[v])
        copy.start()
        waits.append(copy)
    arrivals = []
    for step in range(half):
        for v in range(2):
            for way in range(2):
                if step >= reach(chips, way, v):
                    continue
                index = at(-(step + 1) * (1 - 2 * way))
                block = out_ref.at[index, v]
                ring(way, step, v, block, index).wait_recv()
                if step + 1 < reach(chips, way, v):
                    copy = ring(way, step + 1, v, block, index)
                    copy.start()
                    waits.append(copy)
                copy = sibling(way, step, v, block, index)
                copy.start()
                waits.append(copy)
                arrivals.append(sibling(way, step, v, block, index + flip))
    for v in range(2):
        arrivals.append(sibling(0, half, v, own.at[v], me + flip))
    for copy in arrivals:
        copy.wait_recv()
    for copy in waits:
        if hasattr(copy, "wait_send") and copy.is_remote:
            copy.wait_send()
        else:
            copy.wait()


def gather(chips, dims, wave):
    half = chips // 2
    size = wave.shape[-1]
    sems = pltpu.SemaphoreType.DMA((2, half + 1, 2))
    return pl.pallas_call(
        functools.partial(gather_kernel, chips),
        out_shape=jax.ShapeDtypeStruct((2 * chips, 2, size, size), jnp.bfloat16),
        in_specs=[pl.BlockSpec(memory_space=pltpu.SMEM), pl.BlockSpec(memory_space=pltpu.VMEM)],
        out_specs=pl.BlockSpec(memory_space=pl.ANY),
        scratch_shapes=[
            pltpu.VMEM((2, size, size), jnp.bfloat16),
            pltpu.SemaphoreType.DMA((2,)),
            sems,
            sems,
            sems,
            sems,
        ],
        compiler_params=pltpu.CompilerParams(
            collective_id=0, has_side_effects=True, vmem_limit_bytes=16 * 2**20
        ),
        name="gather",
    )(dims, wave)


def pairs_kernel(src_ref, dst_ref, left_ref, right_ref, wave_ref, out_ref, acc):
    step = pl.program_id(0)

    @pl.when(step == 0)
    def _():
        acc[...] = jnp.zeros_like(acc)

    for g in range(GROUP):
        src = src_ref[step * GROUP + g]
        dst = dst_ref[step * GROUP + g]
        left = left_ref[g]
        right = right_ref[g]
        for v in range(2):
            half = jnp.dot(left, wave_ref[src, v], preferred_element_type=jnp.float32).astype(jnp.bfloat16)
            acc[dst, v] += lax.dot_general(
                half, right, (((1,), (1,)), ((), ())), preferred_element_type=jnp.float32
            )

    @pl.when(step == pl.num_programs(0) - 1)
    def _():
        out_ref[...] = acc[...].astype(jnp.bfloat16)


def pairs(srcs, dsts, lefts, rights, gathered):
    count, size, _ = lefts.shape
    whole = lambda i, s, d: (0, 0, 0, 0)
    block = pl.BlockSpec((GROUP, size, size), lambda i, s, d: (i, 0, 0))
    return pl.pallas_call(
        pairs_kernel,
        out_shape=jax.ShapeDtypeStruct(gathered.shape, jnp.bfloat16),
        grid_spec=pltpu.PrefetchScalarGridSpec(
            num_scalar_prefetch=2,
            grid=(count // GROUP,),
            in_specs=[
                block,
                block,
                pl.BlockSpec(gathered.shape, whole, pipeline_mode=pl.Buffered(1)),
            ],
            out_specs=pl.BlockSpec(gathered.shape, whole, pipeline_mode=pl.Buffered(1)),
            scratch_shapes=[pltpu.VMEM(gathered.shape, jnp.float32)],
        ),
        compiler_params=pltpu.CompilerParams(vmem_limit_bytes=48 * 2**20),
        name="pairs",
    )(srcs, dsts, lefts, rights, gathered)


def scatter_kernel(chips, dims_ref, part_ref, out_ref, sent, came, shared, ring_send, ring_recv, sib_send, sib_recv):
    size = out_ref.shape[-1]
    me, core, at, sib = places(chips)
    flip = 1 - 2 * core
    greet((at(1), at(-1), sib))
    waits = []
    half = chips // 2

    def sibling(way, step, v, index):
        return pltpu.make_async_remote_copy(
            src_ref=part_ref.at[index + flip, v],
            dst_ref=shared.at[way, step, v],
            send_sem=sib_send.at[way, step, v],
            recv_sem=sib_recv.at[way, step, v],
            device_id={"term": sib},
            device_id_type=MESH,
        )

    def ring(way, step, v):
        return pltpu.make_async_remote_copy(
            src_ref=sent.at[way, step, v],
            dst_ref=came.at[way, step, v],
            send_sem=ring_send.at[way, step, v],
            recv_sem=ring_recv.at[way, step, v],
            device_id={"term": at(1 - 2 * way)},
            device_id_type=MESH,
        )

    plan = []
    for step in range(half):
        for v in range(2):
            for way in range(2):
                first = half - reach(chips, way, v)
                if step >= first:
                    index = at((half - step) * (1 - 2 * way))
                    plan.append((way, step, v, first, index))
    for way, step, v, first, index in plan:
        copy = sibling(way, step, v, index)
        copy.start()
        waits.append(copy)
    for v in range(2):
        copy = sibling(0, half, v, me)
        copy.start()
        waits.append(copy)
    for way, step, v, first, index in plan:
        sibling(way, step, v, index).wait_recv()
        total = part_ref[index, v].astype(jnp.float32) + shared[way, step, v].astype(jnp.float32)
        if step > first:
            ring(way, step - 1, v).wait_recv()
            total += came[way, step - 1, v].astype(jnp.float32)
        sent[way, step, v] = total.astype(jnp.bfloat16)
        copy = ring(way, step, v)
        copy.start()
        waits.append(copy)
    mask = mask_of(dims_ref, me, size)
    for v in range(2):
        sibling(0, half, v, me).wait_recv()
        total = part_ref[me, v].astype(jnp.float32) + shared[0, half, v].astype(jnp.float32)
        for way in range(2):
            ring(way, half - 1, v).wait_recv()
            total += came[way, half - 1, v].astype(jnp.float32)
        out_ref[0, v] = (total * mask).astype(jnp.bfloat16)
    for copy in waits:
        copy.wait_send()


def scatter(chips, dims, part):
    half = chips // 2
    size = part.shape[-1]
    sems = pltpu.SemaphoreType.DMA((2, half + 1, 2))
    return pl.pallas_call(
        functools.partial(scatter_kernel, chips),
        out_shape=jax.ShapeDtypeStruct((1, 2, size, size), jnp.bfloat16),
        in_specs=[pl.BlockSpec(memory_space=pltpu.SMEM), pl.BlockSpec(memory_space=pltpu.VMEM)],
        out_specs=pl.BlockSpec(memory_space=pltpu.VMEM),
        scratch_shapes=[
            pltpu.VMEM((2, half, 2, size, size), jnp.bfloat16),
            pltpu.VMEM((2, half, 2, size, size), jnp.bfloat16),
            pltpu.VMEM((2, half + 1, 2, size, size), jnp.bfloat16),
            sems,
            sems,
            sems,
            sems,
        ],
        compiler_params=pltpu.CompilerParams(
            collective_id=1, has_side_effects=True, vmem_limit_bytes=48 * 2**20
        ),
        name="scatter",
    )(dims, part)


def per_device(chips, wave, left_ops, right_ops, pair_src, pair_dst, sector_dims):
    size = wave.shape[-1]
    gathered = gather(chips, sector_dims, wave)
    part = pairs(
        pair_src.reshape(-1),
        pair_dst.reshape(-1),
        left_ops.reshape(-1, size, size),
        right_ops.reshape(-1, size, size),
        gathered,
    )
    return scatter(chips, sector_dims, part)


def solution(mesh):
    held = P(("mol", "term"), None, None, None)
    index = P(("mol", "term"), None)
    return jax.shard_map(
        functools.partial(per_device, mesh.shape["term"] // 2),
        mesh=mesh,
        in_specs=(held, held, held, index, index, P(None, "mol")),
        out_specs=held,
        check_vma=False,
    )
```

```python
import functools

import jax
import jax.numpy as jnp
from jax import lax
from jax.experimental import pallas as pl
from jax.experimental.pallas import tpu as pltpu
from jax.sharding import PartitionSpec as P

MESH = pl.DeviceIdType.MESH
GROUP = 4
LAG = 2


def chip_of(pos, chips):
    if chips == 8:
        back = pos // 4
        return 2 * (pos + back * (7 - 2 * pos)) + back
    return pos


def pos_of(chip, chips):
    if chips == 8:
        up, col = chip // 2, chip % 2
        return up + col * (7 - 2 * up)
    return chip


def places(chips):
    me = lax.axis_index("term")
    core = lax.rem(me, 2)
    pos = pos_of(me // 2, chips)

    def at(shift):
        return 2 * chip_of(lax.rem(pos + shift + chips, chips), chips) + core

    return me, core, at, me + 1 - 2 * core


def greet(devices):
    barrier = pltpu.get_barrier_semaphore()
    for device in devices:
        pl.semaphore_signal(barrier, inc=1, device_id={"term": device}, device_id_type=MESH)
    pl.semaphore_wait(barrier, len(devices))


def reach(chips, way, v):
    return chips // 2 - (1 if way != v else 0)


def kernel(chips, count, table_ref, wave_ref, left_hbm, right_hbm, out_ref,
           wave_in, lefts, rights, got0, got1, sums, own, other, shared, sent, came,
           load_sem, ag_send, ag_recv, ag_sib_send, ag_sib_recv, rs_send, rs_recv, rs_sib_send, rs_sib_recv):
    size = out_ref.shape[-1]
    half = chips // 2
    got = (got0, got1)
    me, core, at, sib = places(chips)
    flip = 1 - 2 * core
    waits = []

    def begin(copy):
        copy.start()
        waits.append(copy)

    loads = [
        pltpu.make_async_copy(wave_ref.at[0], wave_in, load_sem.at[0]),
        pltpu.make_async_copy(left_hbm, lefts, load_sem.at[1]),
        pltpu.make_async_copy(right_hbm, rights, load_sem.at[2]),
    ]
    for copy in loads:
        copy.start()
    greet((at(1), at(-1), sib))

    rows = lax.broadcasted_iota(jnp.int32, (size, size), 0)
    cols = lax.broadcasted_iota(jnp.int32, (size, size), 1)
    dims = 2 * count + 2 * chips
    inside = (rows < table_ref[dims + me]) & (cols < table_ref[dims + 2 * chips + me])
    mask = jnp.where(inside, 1.0, 0.0).astype(jnp.float32)

    def ag_ring(way, step, v, index):
        return pltpu.make_async_remote_copy(
            src_ref=got[v].at[index],
            dst_ref=got[v].at[index],
            send_sem=ag_send.at[way, step, v],
            recv_sem=ag_recv.at[way, step, v],
            device_id={"term": at(1 - 2 * way)},
            device_id_type=MESH,
        )

    def ag_sibling(way, step, v, index):
        return pltpu.make_async_remote_copy(
            src_ref=got[v].at[index],
            dst_ref=got[v].at[index],
            send_sem=ag_sib_send.at[way, step, v],
            recv_sem=ag_sib_recv.at[way, step, v],
            device_id={"term": sib},
            device_id_type=MESH,
        )

    def ag_open(v):
        got[v][me] = (wave_in[v].astype(jnp.float32) * mask).astype(jnp.bfloat16)
        for way in range(2):
            begin(ag_ring(way, 0, v, me))
        begin(ag_sibling(0, half, v, me))

    def ag_event(way, step, v):
        index = at(-(step + 1) * (1 - 2 * way))
        ag_ring(way, step, v, index).wait_recv()
        if step + 1 < reach(chips, way, v):
            begin(ag_ring(way, step + 1, v, index))
        begin(ag_sibling(way, step, v, index))

    def ag_plan(v):
        return [(way, step, v) for step in range(half) for way in (v, 1 - v) if step < reach(chips, way, v)]

    def ag_close(v):
        for way, step, _ in ag_plan(v):
            ag_sibling(way, step, v, at(-(step + 1) * (1 - 2 * way)) + flip).wait_recv()
        ag_sibling(0, half, v, me + flip).wait_recv()

    def rs_sibling(slot, v):
        return pltpu.make_async_remote_copy(
            src_ref=other.at[v, slot],
            dst_ref=shared.at[v, slot],
            send_sem=rs_sib_send.at[v, slot],
            recv_sem=rs_sib_recv.at[v, slot],
            device_id={"term": sib},
            device_id_type=MESH,
        )

    def rs_ring(way, step, v):
        return pltpu.make_async_remote_copy(
            src_ref=sent.at[way, step, v],
            dst_ref=came.at[way, step, v],
            send_sem=rs_send.at[way, step, v],
            recv_sem=rs_recv.at[way, step, v],
            device_id={"term": at(1 - 2 * way)},
            device_id_type=MESH,
        )

    def rs_plan(v):
        plan = []
        for step in range(half):
            for way in (v, 1 - v):
                first = half - reach(chips, way, v)
                if step >= first:
                    plan.append((len(plan), way, step, first, v))
        return plan

    def rs_open(v):
        places_of = [at((half - step) * (1 - 2 * way)) for _, way, step, _, _ in rs_plan(v)] + [me]
        for slot, index in enumerate(places_of):
            other[v, slot] = sums[table_ref[2 * count + index + flip]].astype(jnp.bfloat16)
            begin(rs_sibling(slot, v))
        for slot, index in enumerate(places_of):
            own[v, slot] = sums[table_ref[2 * count + index]]

    def rs_event(slot, way, step, first, v):
        rs_sibling(slot, v).wait_recv()
        total = own[v, slot] + shared[v, slot].astype(jnp.float32)
        if step > first:
            rs_ring(way, step - 1, v).wait_recv()
            total += came[way, step - 1, v].astype(jnp.float32)
        sent[way, step, v] = total.astype(jnp.bfloat16)
        begin(rs_ring(way, step, v))

    def rs_close(v):
        rs_sibling(chips - 1, v).wait_recv()
        total = own[v, chips - 1] + shared[v, chips - 1].astype(jnp.float32)
        for way in range(2):
            rs_ring(way, half - 1, v).wait_recv()
            total += came[way, half - 1, v].astype(jnp.float32)
        out_ref[0, v] = (total * mask).astype(jnp.bfloat16)

    def products(v, first, last):
        @pl.loop(first, last)
        def _(step):
            for g in range(GROUP):
                p = step * GROUP + g
                half_product = jnp.dot(
                    lefts[p], got[v][table_ref[p]], preferred_element_type=jnp.float32
                ).astype(jnp.bfloat16)
                full = lax.dot_general(
                    half_product, rights[p], (((1,), (1,)), ((), ())), preferred_element_type=jnp.float32
                )
                sums[p + 1] = full + sums[table_ref[count + p]]

    def products_beside(v, events):
        groups = count // GROUP
        cuts = [groups * i // (len(events) + 1) for i in range(len(events) + 2)]
        for i in range(len(events) + 1):
            if cuts[i + 1] > cuts[i]:
                products(v, cuts[i], cuts[i + 1])
            if i < len(events):
                events[i]()

    loads[0].wait()
    ag_open(0)
    sums[0] = jnp.zeros((size, size), jnp.float32)
    late = ag_plan(1)
    for step in range(half):
        for item in ag_plan(0):
            if item[1] == step:
                ag_event(*item)
        if step == LAG - 1:
            ag_open(1)
        if step >= LAG:
            for item in ag_plan(1):
                if item[1] == step - LAG:
                    ag_event(*item)
                    late.remove(item)
    ag_close(0)
    loads[1].wait()
    loads[2].wait()
    products_beside(0, [functools.partial(ag_event, *item) for item in late])
    rs_open(0)
    ag_close(1)
    products_beside(1, [functools.partial(rs_event, *item) for item in rs_plan(0)])
    rs_open(1)
    for item in rs_plan(1):
        rs_event(*item)
    for v in range(2):
        rs_close(v)
    for copy in waits:
        copy.wait_send()


def call(chips, table, wave, lefts, rights):
    half = chips // 2
    count, size, _ = lefts.shape
    dma = pltpu.SemaphoreType.DMA
    block = (size, size)
    anywhere = pl.BlockSpec(memory_space=pl.ANY)
    return pl.pallas_call(
        functools.partial(kernel, chips, count),
        out_shape=jax.ShapeDtypeStruct((1, 2) + block, jnp.bfloat16),
        in_specs=[pl.BlockSpec(memory_space=pltpu.SMEM), anywhere, anywhere, anywhere],
        out_specs=pl.BlockSpec(memory_space=pltpu.VMEM),
        scratch_shapes=[
            pltpu.VMEM((2,) + block, jnp.bfloat16),
            pltpu.VMEM((count,) + block, jnp.bfloat16),
            pltpu.VMEM((count,) + block, jnp.bfloat16),
            pltpu.VMEM((2 * chips,) + block, jnp.bfloat16),
            pltpu.VMEM((2 * chips,) + block, jnp.bfloat16),
            pltpu.VMEM((count + 1,) + block, jnp.float32),
            pltpu.VMEM((2, chips) + block, jnp.float32),
            pltpu.VMEM((2, chips) + block, jnp.bfloat16),
            pltpu.VMEM((2, chips) + block, jnp.bfloat16),
            pltpu.VMEM((2, half, 2) + block, jnp.bfloat16),
            pltpu.VMEM((2, half, 2) + block, jnp.bfloat16),
            dma((3,)),
            dma((2, half, 2)),
            dma((2, half, 2)),
            dma((2, half + 1, 2)),
            dma((2, half + 1, 2)),
            dma((2, half, 2)),
            dma((2, half, 2)),
            dma((2, chips)),
            dma((2, chips)),
        ],
        compiler_params=pltpu.CompilerParams(
            collective_id=0, has_side_effects=True, vmem_limit_bytes=61 * 2**20
        ),
        name="davidson",
    )(table, wave, lefts, rights)


def per_device(chips, wave, left_ops, right_ops, pair_src, pair_dst, sector_dims):
    size = wave.shape[-1]
    srcs = pair_src.reshape(-1)
    dsts = pair_dst.reshape(-1)
    count = srcs.shape[0]
    order = jnp.arange(count, dtype=jnp.int32)
    earlier = (dsts[:, None] == dsts[None, :]) & (order[None, :] < order[:, None])
    prev = jnp.max(jnp.where(earlier, order[None, :] + 1, 0), axis=1)
    ends = dsts[None, :] == jnp.arange(2 * chips, dtype=jnp.int32)[:, None]
    last = jnp.max(jnp.where(ends, order[None, :] + 1, 0), axis=1)
    table = jnp.concatenate([srcs, prev, last, sector_dims.reshape(-1)])
    return call(
        chips, table, wave, left_ops.reshape(-1, size, size), right_ops.reshape(-1, size, size)
    )


def solution(mesh):
    held = P(("mol", "term"), None, None, None)
    index = P(("mol", "term"), None)
    return jax.shard_map(
        functools.partial(per_device, mesh.shape["term"] // 2),
        mesh=mesh,
        in_specs=(held, held, held, index, index, P(None, "mol")),
        out_specs=held,
        check_vma=False,
    )
```

```python
import functools

import jax
import jax.numpy as jnp
from jax import lax
from jax.experimental import pallas as pl
from jax.experimental.pallas import tpu as pltpu
from jax.sharding import PartitionSpec as P

MESH = pl.DeviceIdType.MESH
GROUP = 4
LAG = 1
CUTS = 2


def chip_of(pos, chips):
    if chips == 8:
        back = pos // 4
        return 2 * (pos + back * (7 - 2 * pos)) + back
    return pos


def pos_of(chip, chips):
    if chips == 8:
        up, col = chip // 2, chip % 2
        return up + col * (7 - 2 * up)
    return chip


def places(chips):
    me = lax.axis_index("term")
    core = lax.rem(me, 2)
    pos = pos_of(me // 2, chips)

    def at(shift):
        return 2 * chip_of(lax.rem(pos + shift + chips, chips), chips) + core

    return me, core, at, me + 1 - 2 * core


def greet(devices):
    barrier = pltpu.get_barrier_semaphore()
    for device in devices:
        pl.semaphore_signal(barrier, inc=1, device_id={"term": device}, device_id_type=MESH)
    pl.semaphore_wait(barrier, len(devices))


def reach(chips, way, v):
    return chips // 2 - (1 if way != v else 0)


def kernel(chips, count, table_ref, wave_ref, left_hbm, right_hbm, out_ref,
           wave_in, lefts, rights, got0, got1, sums, own, other, shared, sent, came,
           load_sem, ag_send, ag_recv, ag_sib_send, ag_sib_recv, rs_send, rs_recv, rs_sib_send, rs_sib_recv):
    size = out_ref.shape[-1]
    half = chips // 2
    got = (got0, got1)
    me, core, at, sib = places(chips)
    flip = 1 - 2 * core
    waits = []

    def begin(copy):
        copy.start()
        waits.append(copy)

    loads = [
        pltpu.make_async_copy(wave_ref.at[0], wave_in, load_sem.at[0]),
        pltpu.make_async_copy(left_hbm, lefts, load_sem.at[1]),
        pltpu.make_async_copy(right_hbm, rights, load_sem.at[2]),
    ]
    for copy in loads:
        copy.start()
    greet((at(1), at(-1), sib))

    rows = lax.broadcasted_iota(jnp.int32, (size, size), 0)
    cols = lax.broadcasted_iota(jnp.int32, (size, size), 1)
    dims = 2 * count + 2 * chips
    inside = (rows < table_ref[dims + me]) & (cols < table_ref[dims + 2 * chips + me])
    mask = jnp.where(inside, 1.0, 0.0).astype(jnp.float32)

    def cut(r):
        return pl.ds(r * (size // CUTS), size // CUTS)

    def ag_ring(way, step, v, index, r):
        return pltpu.make_async_remote_copy(
            src_ref=got[v].at[index, cut(r)],
            dst_ref=got[v].at[index, cut(r)],
            send_sem=ag_send.at[way, step, v, r],
            recv_sem=ag_recv.at[way, step, v, r],
            device_id={"term": at(1 - 2 * way)},
            device_id_type=MESH,
        )

    def ag_sibling(way, step, v, index):
        return pltpu.make_async_remote_copy(
            src_ref=got[v].at[index],
            dst_ref=got[v].at[index],
            send_sem=ag_sib_send.at[way, step, v],
            recv_sem=ag_sib_recv.at[way, step, v],
            device_id={"term": sib},
            device_id_type=MESH,
        )

    def ag_open(v):
        got[v][me] = (wave_in[v].astype(jnp.float32) * mask).astype(jnp.bfloat16)
        for r in range(CUTS):
            for way in range(2):
                begin(ag_ring(way, 0, v, me, r))
        begin(ag_sibling(0, half, v, me))

    def ag_event(way, step, v, r):
        index = at(-(step + 1) * (1 - 2 * way))
        ag_ring(way, step, v, index, r).wait_recv()
        if step + 1 < reach(chips, way, v):
            begin(ag_ring(way, step + 1, v, index, r))
        if r == CUTS - 1:
            begin(ag_sibling(way, step, v, index))

    def ag_plan(v):
        return [
            (way, step, v, r)
            for step in range(half)
            for r in range(CUTS)
            for way in (v, 1 - v)
            if step < reach(chips, way, v)
        ]

    def ag_close(v):
        for way, step, _, r in ag_plan(v):
            if r == 0:
                ag_sibling(way, step, v, at(-(step + 1) * (1 - 2 * way)) + flip).wait_recv()
        ag_sibling(0, half, v, me + flip).wait_recv()

    def rs_sibling(slot, v):
        return pltpu.make_async_remote_copy(
            src_ref=other.at[v, slot],
            dst_ref=shared.at[v, slot],
            send_sem=rs_sib_send.at[v, slot],
            recv_sem=rs_sib_recv.at[v, slot],
            device_id={"term": sib},
            device_id_type=MESH,
        )

    def rs_ring(way, step, v, r):
        return pltpu.make_async_remote_copy(
            src_ref=sent.at[way, step, v, cut(r)],
            dst_ref=came.at[way, step, v, cut(r)],
            send_sem=rs_send.at[way, step, v, r],
            recv_sem=rs_recv.at[way, step, v, r],
            device_id={"term": at(1 - 2 * way)},
            device_id_type=MESH,
        )

    def rs_plan(v):
        plan = []
        for step in range(half):
            for way in (v, 1 - v):
                first = half - reach(chips, way, v)
                if step >= first:
                    plan.append((len(plan), way, step, first, v))
        return plan

    def rs_open(v):
        places_of = [at((half - step) * (1 - 2 * way)) for _, way, step, _, _ in rs_plan(v)] + [me]
        for slot, index in enumerate(places_of):
            other[v, slot] = sums[table_ref[2 * count + index + flip]].astype(jnp.bfloat16)
            begin(rs_sibling(slot, v))
        for slot, index in enumerate(places_of):
            own[v, slot] = sums[table_ref[2 * count + index]]

    def rs_event(slot, way, step, first, v, r):
        if r == 0:
            rs_sibling(slot, v).wait_recv()
        total = own[v, slot, cut(r)] + shared[v, slot, cut(r)].astype(jnp.float32)
        if step > first:
            rs_ring(way, step - 1, v, r).wait_recv()
            total += came[way, step - 1, v, cut(r)].astype(jnp.float32)
        sent[way, step, v, cut(r)] = total.astype(jnp.bfloat16)
        begin(rs_ring(way, step, v, r))

    def rs_events(v, steps):
        plan = [item for item in rs_plan(v) if item[2] in steps]
        return [
            functools.partial(rs_event, *item, r)
            for step in steps
            for r in range(CUTS)
            for item in plan
            if item[2] == step
        ]

    def rs_close(v):
        rs_sibling(chips - 1, v).wait_recv()
        total = own[v, chips - 1] + shared[v, chips - 1].astype(jnp.float32)
        for way in range(2):
            for r in range(CUTS):
                rs_ring(way, half - 1, v, r).wait_recv()
            total += came[way, half - 1, v].astype(jnp.float32)
        out_ref[0, v] = (total * mask).astype(jnp.bfloat16)

    def products(v, first, last):
        @pl.loop(first, last)
        def _(step):
            for g in range(GROUP):
                p = step * GROUP + g
                half_product = jnp.dot(
                    lefts[p], got[v][table_ref[p]], preferred_element_type=jnp.float32
                ).astype(jnp.bfloat16)
                full = lax.dot_general(
                    half_product, rights[p], (((1,), (1,)), ((), ())), preferred_element_type=jnp.float32
                )
                sums[p + 1] = full + sums[table_ref[count + p]]

    def products_beside(v, events):
        groups = count // GROUP
        cuts = [groups * i // (len(events) + 1) for i in range(len(events) + 2)]
        for i in range(len(events) + 1):
            if cuts[i + 1] > cuts[i]:
                products(v, cuts[i], cuts[i + 1])
            if i < len(events):
                events[i]()

    loads[0].wait()
    ag_open(0)
    sums[0] = jnp.zeros((size, size), jnp.float32)
    late = ag_plan(1)
    for step in range(half):
        for item in ag_plan(0):
            if item[1] == step:
                ag_event(*item)
        if step == LAG - 1:
            ag_open(1)
        if step >= LAG:
            for item in ag_plan(1):
                if item[1] == step - LAG:
                    ag_event(*item)
                    late.remove(item)
    ag_close(0)
    loads[1].wait()
    loads[2].wait()
    products_beside(0, [functools.partial(ag_event, *item) for item in late])
    rs_open(0)
    ag_close(1)
    early = half // 2 + 1
    products_beside(1, rs_events(0, range(early)))
    rs_open(1)
    for step in range(half):
        if step + early < half:
            for event in rs_events(0, [step + early]):
                event()
        for event in rs_events(1, [step]):
            event()
    for v in range(2):
        rs_close(v)
    for copy in waits:
        copy.wait_send()


def call(chips, table, wave, lefts, rights):
    half = chips // 2
    count, size, _ = lefts.shape
    dma = pltpu.SemaphoreType.DMA
    block = (size, size)
    anywhere = pl.BlockSpec(memory_space=pl.ANY)
    return pl.pallas_call(
        functools.partial(kernel, chips, count),
        out_shape=jax.ShapeDtypeStruct((1, 2) + block, jnp.bfloat16),
        in_specs=[pl.BlockSpec(memory_space=pltpu.SMEM), anywhere, anywhere, anywhere],
        out_specs=pl.BlockSpec(memory_space=pltpu.VMEM),
        scratch_shapes=[
            pltpu.VMEM((2,) + block, jnp.bfloat16),
            pltpu.VMEM((count,) + block, jnp.bfloat16),
            pltpu.VMEM((count,) + block, jnp.bfloat16),
            pltpu.VMEM((2 * chips,) + block, jnp.bfloat16),
            pltpu.VMEM((2 * chips,) + block, jnp.bfloat16),
            pltpu.VMEM((count + 1,) + block, jnp.float32),
            pltpu.VMEM((2, chips) + block, jnp.float32),
            pltpu.VMEM((2, chips) + block, jnp.bfloat16),
            pltpu.VMEM((2, chips) + block, jnp.bfloat16),
            pltpu.VMEM((2, half, 2) + block, jnp.bfloat16),
            pltpu.VMEM((2, half, 2) + block, jnp.bfloat16),
            dma((3,)),
            dma((2, half, 2, CUTS)),
            dma((2, half, 2, CUTS)),
            dma((2, half + 1, 2)),
            dma((2, half + 1, 2)),
            dma((2, half, 2, CUTS)),
            dma((2, half, 2, CUTS)),
            dma((2, chips)),
            dma((2, chips)),
        ],
        compiler_params=pltpu.CompilerParams(
            collective_id=0, has_side_effects=True, vmem_limit_bytes=61 * 2**20
        ),
        name="davidson",
    )(table, wave, lefts, rights)


def per_device(chips, wave, left_ops, right_ops, pair_src, pair_dst, sector_dims):
    size = wave.shape[-1]
    srcs = pair_src.reshape(-1)
    dsts = pair_dst.reshape(-1)
    count = srcs.shape[0]
    order = jnp.arange(count, dtype=jnp.int32)
    earlier = (dsts[:, None] == dsts[None, :]) & (order[None, :] < order[:, None])
    prev = jnp.max(jnp.where(earlier, order[None, :] + 1, 0), axis=1)
    ends = dsts[None, :] == jnp.arange(2 * chips, dtype=jnp.int32)[:, None]
    last = jnp.max(jnp.where(ends, order[None, :] + 1, 0), axis=1)
    table = jnp.concatenate([srcs, prev, last, sector_dims.reshape(-1)])
    return call(
        chips, table, wave, left_ops.reshape(-1, size, size), right_ops.reshape(-1, size, size)
    )


def solution(mesh):
    held = P(("mol", "term"), None, None, None)
    index = P(("mol", "term"), None)
    return jax.shard_map(
        functools.partial(per_device, mesh.shape["term"] // 2),
        mesh=mesh,
        in_specs=(held, held, held, index, index, P(None, "mol")),
        out_specs=held,
        check_vma=False,
    )
```

```python
import functools

import jax
import jax.numpy as jnp
from jax import lax
from jax.experimental import pallas as pl
from jax.experimental.pallas import tpu as pltpu
from jax.sharding import PartitionSpec as P

MESH = pl.DeviceIdType.MESH
GROUP = 4
LAG = 1
CUTS = 4


def chip_of(pos, chips):
    if chips == 8:
        back = pos // 4
        return 2 * (pos + back * (7 - 2 * pos)) + back
    return pos


def pos_of(chip, chips):
    if chips == 8:
        up, col = chip // 2, chip % 2
        return up + col * (7 - 2 * up)
    return chip


def places(chips):
    me = lax.axis_index("term")
    core = lax.rem(me, 2)
    pos = pos_of(me // 2, chips)

    def at(shift):
        return 2 * chip_of(lax.rem(pos + shift + chips, chips), chips) + core

    return me, core, at, me + 1 - 2 * core


def greet(devices):
    barrier = pltpu.get_barrier_semaphore()
    for device in devices:
        pl.semaphore_signal(barrier, inc=1, device_id={"term": device}, device_id_type=MESH)
    pl.semaphore_wait(barrier, len(devices))


def reach(chips, way, v):
    return chips // 2 - (1 if way != v else 0)


def kernel(chips, count, src_ref, dims_ref, table_ref, wave_ref, left_hbm, right_hbm, out_ref,
           wave_in, lefts, rights, got0, got1, sums, own, other, shared, sent, came,
           load_sem, ag_send, ag_recv, ag_sib_send, ag_sib_recv, rs_send, rs_recv, rs_sib_send, rs_sib_recv):
    size = out_ref.shape[-1]
    half = chips // 2
    got = (got0, got1)
    me, core, at, sib = places(chips)
    flip = 1 - 2 * core
    row = src_ref.shape[1]
    waits = []

    def begin(copy):
        copy.start()
        waits.append(copy)

    loads = [
        pltpu.make_async_copy(wave_ref.at[0], wave_in, load_sem.at[0]),
        pltpu.make_async_copy(left_hbm, lefts, load_sem.at[1]),
        pltpu.make_async_copy(right_hbm, rights, load_sem.at[2]),
    ]
    for copy in loads:
        copy.start()
    greet((at(1), at(-1), sib))

    rows = lax.broadcasted_iota(jnp.int32, (size, size), 0)
    cols = lax.broadcasted_iota(jnp.int32, (size, size), 1)
    inside = (rows < dims_ref[0, me]) & (cols < dims_ref[1, me])
    mask = jnp.where(inside, 1.0, 0.0).astype(jnp.float32)

    def cut(r):
        return pl.ds(r * (size // CUTS), size // CUTS)

    def ag_ring(way, step, v, index, r):
        return pltpu.make_async_remote_copy(
            src_ref=got[v].at[index, cut(r)],
            dst_ref=got[v].at[index, cut(r)],
            send_sem=ag_send.at[way, step, v, r],
            recv_sem=ag_recv.at[way, step, v, r],
            device_id={"term": at(1 - 2 * way)},
            device_id_type=MESH,
        )

    def ag_sibling(way, step, v, index):
        return pltpu.make_async_remote_copy(
            src_ref=got[v].at[index],
            dst_ref=got[v].at[index],
            send_sem=ag_sib_send.at[way, step, v],
            recv_sem=ag_sib_recv.at[way, step, v],
            device_id={"term": sib},
            device_id_type=MESH,
        )

    def ag_open(v):
        got[v][me] = (wave_in[v].astype(jnp.float32) * mask).astype(jnp.bfloat16)
        for r in range(CUTS):
            for way in range(2):
                begin(ag_ring(way, 0, v, me, r))
        begin(ag_sibling(0, half, v, me))

    def ag_event(way, step, v, r):
        index = at(-(step + 1) * (1 - 2 * way))
        ag_ring(way, step, v, index, r).wait_recv()
        if step + 1 < reach(chips, way, v):
            begin(ag_ring(way, step + 1, v, index, r))
        if r == CUTS - 1:
            begin(ag_sibling(way, step, v, index))

    def ag_plan(v):
        return [
            (way, step, v, r)
            for step in range(half)
            for r in range(CUTS)
            for way in (v, 1 - v)
            if step < reach(chips, way, v)
        ]

    def ag_close(v):
        for way, step, _, r in ag_plan(v):
            if r == 0:
                ag_sibling(way, step, v, at(-(step + 1) * (1 - 2 * way)) + flip).wait_recv()
        ag_sibling(0, half, v, me + flip).wait_recv()

    def rs_sibling(slot, v):
        return pltpu.make_async_remote_copy(
            src_ref=other.at[v, slot],
            dst_ref=shared.at[v, slot],
            send_sem=rs_sib_send.at[v, slot],
            recv_sem=rs_sib_recv.at[v, slot],
            device_id={"term": sib},
            device_id_type=MESH,
        )

    def rs_ring(way, step, v, r):
        return pltpu.make_async_remote_copy(
            src_ref=sent.at[way, step, v, cut(r)],
            dst_ref=came.at[way, step, v, cut(r)],
            send_sem=rs_send.at[way, step, v, r],
            recv_sem=rs_recv.at[way, step, v, r],
            device_id={"term": at(1 - 2 * way)},
            device_id_type=MESH,
        )

    def rs_plan(v):
        plan = []
        for step in range(half):
            for way in (v, 1 - v):
                first = half - reach(chips, way, v)
                if step >= first:
                    plan.append((len(plan), way, step, first, v))
        return plan

    def rs_open(v):
        places_of = [at((half - step) * (1 - 2 * way)) for _, way, step, _, _ in rs_plan(v)] + [me]
        for slot, index in enumerate(places_of):
            other[v, slot] = sums[table_ref[count + index + flip]].astype(jnp.bfloat16)
            begin(rs_sibling(slot, v))
        for slot, index in enumerate(places_of):
            own[v, slot] = sums[table_ref[count + index]]

    def rs_event(slot, way, step, first, v, r):
        if r == 0:
            rs_sibling(slot, v).wait_recv()
        total = own[v, slot, cut(r)] + shared[v, slot, cut(r)].astype(jnp.float32)
        if step > first:
            rs_ring(way, step - 1, v, r).wait_recv()
            total += came[way, step - 1, v, cut(r)].astype(jnp.float32)
        sent[way, step, v, cut(r)] = total.astype(jnp.bfloat16)
        begin(rs_ring(way, step, v, r))

    def rs_events(v, steps):
        plan = [item for item in rs_plan(v) if item[2] in steps]
        return [
            functools.partial(rs_event, *item, r)
            for step in steps
            for r in range(CUTS)
            for item in plan
            if item[2] == step
        ]

    def rs_close(v):
        rs_sibling(chips - 1, v).wait_recv()
        total = own[v, chips - 1] + shared[v, chips - 1].astype(jnp.float32)
        for way in range(2):
            for r in range(CUTS):
                rs_ring(way, half - 1, v, r).wait_recv()
            total += came[way, half - 1, v].astype(jnp.float32)
        out_ref[0, v] = (total * mask).astype(jnp.bfloat16)

    def products(v, first, last):
        @pl.loop(first, last)
        def _(step):
            for g in range(GROUP):
                p = step * GROUP + g
                half_product = jnp.dot(
                    lefts[p], got[v][src_ref[p // row, lax.rem(p, row)]], preferred_element_type=jnp.float32
                ).astype(jnp.bfloat16)
                full = lax.dot_general(
                    half_product, rights[p], (((1,), (1,)), ((), ())), preferred_element_type=jnp.float32
                )
                sums[p + 1] = full + sums[table_ref[p]]

    def products_beside(v, events):
        groups = count // GROUP
        cuts = [groups * i // (len(events) + 1) for i in range(len(events) + 2)]
        for i in range(len(events) + 1):
            if cuts[i + 1] > cuts[i]:
                products(v, cuts[i], cuts[i + 1])
            if i < len(events):
                events[i]()

    loads[0].wait()
    ag_open(0)
    sums[0] = jnp.zeros((size, size), jnp.float32)
    late = ag_plan(1)
    for step in range(half):
        for item in ag_plan(0):
            if item[1] == step:
                ag_event(*item)
        if step == LAG - 1:
            ag_open(1)
        if step >= LAG:
            for item in ag_plan(1):
                if item[1] == step - LAG:
                    ag_event(*item)
                    late.remove(item)
    ag_close(0)
    loads[1].wait()
    loads[2].wait()
    products_beside(0, [functools.partial(ag_event, *item) for item in late])
    rs_open(0)
    ag_close(1)
    early = half // 2
    products_beside(1, rs_events(0, range(early)))
    rs_open(1)
    for step in range(half):
        if step + early < half:
            for event in rs_events(0, [step + early]):
                event()
        for event in rs_events(1, [step]):
            event()
    for v in range(2):
        rs_close(v)
    for copy in waits:
        copy.wait_send()


def call(chips, srcs, dims, table, wave, lefts, rights):
    half = chips // 2
    count, size, _ = lefts.shape
    dma = pltpu.SemaphoreType.DMA
    block = (size, size)
    anywhere = pl.BlockSpec(memory_space=pl.ANY)
    return pl.pallas_call(
        functools.partial(kernel, chips, count),
        out_shape=jax.ShapeDtypeStruct((1, 2) + block, jnp.bfloat16),
        in_specs=[pl.BlockSpec(memory_space=pltpu.SMEM)] * 3 + [anywhere] * 3,
        out_specs=pl.BlockSpec(memory_space=pltpu.VMEM),
        scratch_shapes=[
            pltpu.VMEM((2,) + block, jnp.bfloat16),
            pltpu.VMEM((count,) + block, jnp.bfloat16),
            pltpu.VMEM((count,) + block, jnp.bfloat16),
            pltpu.VMEM((2 * chips,) + block, jnp.bfloat16),
            pltpu.VMEM((2 * chips,) + block, jnp.bfloat16),
            pltpu.VMEM((count + 1,) + block, jnp.float32),
            pltpu.VMEM((2, chips) + block, jnp.float32),
            pltpu.VMEM((2, chips) + block, jnp.bfloat16),
            pltpu.VMEM((2, chips) + block, jnp.bfloat16),
            pltpu.VMEM((2, half, 2) + block, jnp.bfloat16),
            pltpu.VMEM((2, half, 2) + block, jnp.bfloat16),
            dma((3,)),
            dma((2, half, 2, CUTS)),
            dma((2, half, 2, CUTS)),
            dma((2, half + 1, 2)),
            dma((2, half + 1, 2)),
            dma((2, half, 2, CUTS)),
            dma((2, half, 2, CUTS)),
            dma((2, chips)),
            dma((2, chips)),
        ],
        compiler_params=pltpu.CompilerParams(
            collective_id=0, has_side_effects=True, vmem_limit_bytes=61 * 2**20
        ),
        name="davidson",
    )(srcs, dims, table, wave, lefts, rights)


def per_device(chips, wave, left_ops, right_ops, pair_src, pair_dst, sector_dims):
    size = wave.shape[-1]
    dsts = pair_dst.reshape(-1)
    count = dsts.shape[0]
    order = jnp.arange(count, dtype=jnp.int32)
    earlier = (dsts[:, None] == dsts[None, :]) & (order[None, :] < order[:, None])
    prev = jnp.max(jnp.where(earlier, order[None, :] + 1, 0), axis=1)
    ends = dsts[None, :] == jnp.arange(2 * chips, dtype=jnp.int32)[:, None]
    last = jnp.max(jnp.where(ends, order[None, :] + 1, 0), axis=1)
    table = jnp.concatenate([prev, last])
    return call(
        chips,
        pair_src,
        sector_dims,
        table,
        wave,
        left_ops.reshape(-1, size, size),
        right_ops.reshape(-1, size, size),
    )


def solution(mesh):
    held = P(("mol", "term"), None, None, None)
    index = P(("mol", "term"), None)
    return jax.shard_map(
        functools.partial(per_device, mesh.shape["term"] // 2),
        mesh=mesh,
        in_specs=(held, held, held, index, index, P(None, "mol")),
        out_specs=held,
        check_vma=False,
    )
```
